32 devices in a mesh: facet: 2 (over x), vis: 8 (over z, core), spec: 2 (over y).
Axes of the slice: x: 2, y: 2, z: 4, core: 2. Of those that a mesh axis runs over, the one named last changes fastest.
Arguments:
- image: float32 [128, 8, 4096], P(('facet', 'vis'), 'spec'), may hold values from 0 to 1
- wavelet_dual: float32 [128, 8, 4096], P(('facet', 'vis'), 'spec'), may hold values from -6 to 6
- weights: float32 [128, 4096], P(('facet', 'vis')), may hold values from 0.3 to 3
- kernels: bfloat16 [2, 8, 2, 256, 64], P('facet', 'vis'), may hold values from -0.5 to 0.5
- vis_data: bfloat16 [2, 8, 8, 2, 16, 256, 128], P('facet', 'vis', 'spec'), may hold values from -6 to 6
- tile_list: int32 [2, 8, 16], P('facet', 'vis'), may hold values from 0 to 31, as said below
- tile_count: int32 [2, 8], P('facet', 'vis'), may hold values from 4 to 16, as said below
Outputs:
- image_next: float32 [128, 8, 4096], P(('facet', 'vis'), 'spec')
- dual_next: float32 [128, 8, 4096], P(('facet', 'vis'), 'spec')
The draws below stay inside these ranges and needn't reach their ends.
Inputs may be any that keep to these rules, and one draw needn't show every extreme that they name: `tile_list`: the 16 slots of a block name distinct tiles; slots from tile_count on are unused. `tile_count`: every draw has a block with 16 occupied slots and one with the fewest allowed.
All inputs are finite; a program needn't handle non-finite values.
Results may differ from the reference program's by a relative error of at most 0.017.
Values may be sent and summed in bfloat16 or wider, within the bound.
A program may use at most 128 MiB of HBM per device.

```python
import math
import jax
import jax.numpy as jnp
from jax import lax

FW = 4096
MVIS = 256
NFAC = 2
NBLK = 8
FROWS = 64
ROWS = 128
CH = 8
NT = 32
KMAX = 16


def one_order(one_key):
    return jax.random.permutation(one_key, NT)


def draw_tile_list(key, part):
    blocks_all = NFAC * NBLK
    keys = jax.random.split(key, blocks_all)
    orders = jax.vmap(one_order)(keys)
    return orders[:, :KMAX].reshape(NFAC, NBLK, KMAX).astype(jnp.int32)


def draw_tile_count(key, part):
    blocks_all = NFAC * NBLK
    fewest = max(1, KMAX // 4)
    spread = KMAX - fewest
    draw_one = jax.random.randint(jax.random.fold_in(key, 1), (blocks_all,), 0, spread + 1)
    draw_two = jax.random.randint(jax.random.fold_in(key, 2), (blocks_all,), 0, spread + 1)
    counts = fewest + jnp.minimum(draw_one, draw_two)
    where_most = jax.random.randint(jax.random.fold_in(key, 3), (), 0, blocks_all)
    counts = counts.at[where_most].set(KMAX)
    counts = counts.at[(where_most + 1) % blocks_all].set(fewest)
    return counts.reshape(NFAC, NBLK).astype(jnp.int32)


def level_of(rng, shape, cuts, least, high):
    def one(dim, parts):
        steps = jax.random.uniform(jax.random.fold_in(jax.random.fold_in(rng, 6), dim), (parts,), jnp.float32, least / len(cuts), high / len(cuts))
        return jnp.repeat(jnp.exp(steps), shape[dim] // parts).reshape((-1,) + (1,) * (len(shape) - dim - 1))

    level = one(*cuts[0])
    for cut in cuts[1:]:
        level = level * one(*cut)
    return level


def scatter_about(rng, extent, deviation, bound, cuts=(), kind=jnp.bfloat16):
    factor_of = level_of(rng, extent, cuts, -0.22, 0.18) if cuts else 1.0
    result = jax.random.normal(rng, extent, jnp.float32) * deviation * factor_of
    return jnp.minimum(jnp.maximum(result, -bound), bound).astype(kind)


def setup_inputs(seed: int = 0) -> dict:
    key_of = jax.random.split(jax.random.key(seed), 8)
    image = jnp.clip(1.0 * jax.random.uniform(key_of[0], (ROWS, CH, FW), jnp.float32) ** level_of(key_of[0], (ROWS, CH, FW), ((0, 16), (1, 2)), -0.2, 0.2), 0.0, 1.0)
    wavelet_dual = scatter_about(key_of[1], (ROWS, CH, FW), 1.0, 6.0, ((0, 16), (1, 2)), jnp.float32)
    weights = jnp.clip(jnp.exp(math.log(3.0) - 2.3025851 * jax.random.uniform(key_of[2], (ROWS, FW), jnp.float32) ** level_of(key_of[2], (ROWS, FW), ((0, 16),), -0.2, 0.2)), 0.3, 3.0)
    kernels = scatter_about(key_of[3], (NFAC, NBLK, 2, MVIS, FROWS), (2 * FROWS) ** -0.5, 0.5, ((0, 2), (1, 8)))
    vis_data = scatter_about(key_of[4], (NFAC, NBLK, CH, 2, KMAX, MVIS, 128), 1.0, 6.0, ((0, 2), (1, 8), (2, 2)))
    tile_list = draw_tile_list(jax.random.fold_in(key_of[7], 71), 0)
    tile_count = draw_tile_count(jax.random.fold_in(key_of[7], 71), 0)
    return {"image": image, "wavelet_dual": wavelet_dual, "weights": weights, "kernels": kernels, "vis_data": vis_data, "tile_list": tile_list, "tile_count": tile_count}


root_three = math.sqrt(3.0)
norm_factor = 4.0 * math.sqrt(2.0)
low_taps = [(1.0 + root_three) / norm_factor, (3.0 + root_three) / norm_factor, (3.0 - root_three) / norm_factor, (1.0 - root_three) / norm_factor]
high_taps = [low_taps[3], -low_taps[2], low_taps[1], -low_taps[0]]
primal_step = 0.2
dual_step = 0.5

def kernel_blocks(kernel_pair):
    real_k = kernel_pair[0]
    imag_k = kernel_pair[1]
    top_row = jnp.stack([real_k, -imag_k], axis=1)
    bottom_row = jnp.stack([imag_k, real_k], axis=1)
    return jnp.stack([top_row, bottom_row], axis=0)

def reference(image, wavelet_dual, weights, kernels, vis_data, tile_list, tile_count):
    unit_scale = 1.0 / math.sqrt(FW)
    spectrum = jnp.fft.fft(image, axis=-1)
    grid = jnp.stack([jnp.real(spectrum), jnp.imag(spectrum)], axis=2) * unit_scale
    grid = lax.optimization_barrier(grid.astype(jnp.bfloat16))
    grid = grid.reshape(NFAC, FROWS, CH, 2, NT, 128)
    columns = jnp.arange(NT, dtype=jnp.int32)
    slot_index = jnp.arange(KMAX, dtype=jnp.int32)

    def facet_sum(packed):
        facet_grid, facet_kernels, facet_data, facet_lists, facet_counts = packed
        grid_wide = facet_grid.astype(jnp.float32)

        def block_step(running, block_args):
            kernel_pair, block_data, block_list, block_count = block_args
            stacked = kernel_blocks(kernel_pair).astype(jnp.float32)
            one_hot = (block_list[:, None] == columns[None, :]).astype(jnp.float32)
            picked = jnp.einsum('rcitn,kt->rcikn', grid_wide, one_hot)
            predicted = jnp.einsum('omir,rcikn->cokmn', stacked, picked)
            live_slots = (slot_index < block_count)[None, None, :, None, None]
            residual = jnp.where(live_slots, predicted - block_data.astype(jnp.float32), 0.0).astype(jnp.bfloat16)
            residual = lax.optimization_barrier(residual)
            partial_tiles = jnp.einsum('omir,cokmn->rcikn', stacked, residual.astype(jnp.float32))
            partial_tiles = lax.optimization_barrier(partial_tiles.astype(jnp.bfloat16))
            placed = jnp.einsum('rcikn,kt->rcitn', partial_tiles.astype(jnp.float32), one_hot)
            return (running + placed, None)
        zero_grid = jnp.zeros((FROWS, CH, 2, NT, 128), jnp.float32)
        facet_total, ignored = lax.scan(block_step, zero_grid, (facet_kernels, facet_data, facet_lists, facet_counts))
        return facet_total
    grid_sums = lax.map(facet_sum, (grid, kernels, vis_data, tile_list, tile_count))
    grid_sums = grid_sums.reshape(ROWS, CH, 2, FW)
    inverse = jnp.fft.ifft(lax.complex(grid_sums[:, :, 0], grid_sums[:, :, 1]), axis=-1)
    gradient = jnp.real(inverse) * (FW * unit_scale)
    padded_dual = jnp.concatenate([jnp.zeros((3, CH, FW), wavelet_dual.dtype), wavelet_dual], axis=0)
    synthesized = jnp.zeros_like(wavelet_dual)
    for offset in range(4):
        synthesized = synthesized + high_taps[offset] * padded_dual[3 - offset:3 - offset + ROWS]
    image_next = jnp.maximum(image - primal_step * (gradient + synthesized), 0.0)
    extrap = 2.0 * image_next - image
    padded_next = jnp.concatenate([extrap, jnp.zeros((3, CH, FW), extrap.dtype)], axis=0)
    detail = jnp.zeros_like(extrap)
    for offset in range(4):
        detail = detail + high_taps[offset] * padded_next[offset:offset + ROWS]
    update = wavelet_dual + dual_step * detail
    energy = lax.optimization_barrier(jnp.sum(update * update, axis=1))
    dual_next = update * weights[:, None, :] / jnp.maximum(weights, jnp.sqrt(energy))[:, None, :]
    return (image_next, dual_next)
```

```python
import functools
import math

import jax
import jax.numpy as jnp
import numpy as np
from jax import lax
from jax.experimental import pallas as pl
from jax.experimental.pallas import tpu as pltpu
from jax.sharding import PartitionSpec as P

MESH = pl.DeviceIdType.MESH
root_three = math.sqrt(3.0)
norm_factor = 4.0 * math.sqrt(2.0)
low_taps = [
    (1.0 + root_three) / norm_factor,
    (3.0 + root_three) / norm_factor,
    (3.0 - root_three) / norm_factor,
    (1.0 - root_three) / norm_factor,
]
high_taps = [low_taps[3], -low_taps[2], low_taps[1], -low_taps[0]]
primal_step = 0.2
dual_step = 0.5
lanes = 128
bf16 = jnp.bfloat16
f32 = jnp.float32


def nn(a, b):
    return jnp.dot(a, b, preferred_element_type=f32)


def nt(a, b):
    return lax.dot_general(a, b, (((1,), (1,)), ((), ())), preferred_element_type=f32)


def tables(rows, chans, width, blocks):
    outer = width // lanes
    half = outer // 2
    tiles = half + 1
    scale = 1.0 / math.sqrt(width)
    one = np.arange(outer)
    small = 2.0 * np.pi * (np.outer(one, one) % outer) / outer
    cos_s, sin_s = np.cos(small), np.sin(small)
    eye_c, eye_r = np.eye(chans), np.eye(rows)
    parts = np.stack([cos_s, -sin_s]) * scale
    fwd_a = np.einsum("pla,cd->cplad", parts, eye_c).reshape(chans * 2 * outer, outer * chans)
    angle = 2.0 * np.pi * (np.outer(np.arange(tiles), np.arange(lanes)) % outer) / outer
    cos_t, sin_t = np.cos(angle), np.sin(angle)
    mix = np.array([[cos_t, sin_t], [-sin_t, cos_t]])
    fwd_b = np.einsum("iptb,rs->tirspb", mix, eye_r).reshape(tiles * 2 * rows, rows * 2 * lanes)
    cos_o, sin_o = cos_t[:, :outer], sin_t[:, :outer]
    mix = np.array([[cos_o, -sin_o], [sin_o, cos_o]])
    inv_t = np.einsum("pitb,rs->rpbtis", mix, eye_r).reshape(rows * 2 * outer, tiles * 2 * rows)
    angle = 2.0 * np.pi * (np.outer(one, np.arange(lanes)) % outer) / outer
    parts = np.stack([np.cos(angle), -np.sin(angle)]) * scale
    inv_l = np.einsum("pal,cd->acdpl", parts, eye_c).reshape(outer * chans, chans * 2 * lanes)
    twist = 2.0 * np.pi * np.outer(np.arange(lanes), np.arange(lanes)) / width
    twist = np.stack([np.cos(twist), np.sin(twist)]).reshape(2, lanes // outer, outer, lanes)
    flip = np.zeros((lanes, lanes))
    for col in range(1, lanes):
        flip[lanes - col, col] = 1.0
    spread = np.zeros((2, blocks, 2, rows, blocks * rows))
    for shard in range(blocks):
        place = (shard % 2) * (blocks // 2) + shard // 2
        for row in range(rows):
            for part in range(2):
                spread[part, place, part, row, shard * rows + row] = 1.0
    spread = spread.reshape(2, blocks * 2 * rows, blocks * rows)
    halves = np.ones((tiles, 2 * rows, lanes))
    halves[0, :, 0] = 0.5
    halves[half, :, 1:] = 0.0
    halves[half, :, 0] = 0.5
    gather_c = np.kron(np.eye(outer), np.ones((1, chans)))

    def b(x):
        return jnp.asarray(x.astype(np.float32), bf16)

    def f(x):
        return jnp.asarray(x.astype(np.float32))

    return [
        b(fwd_a), b(fwd_b), b(inv_t), b(inv_l), f(twist), b(flip), b(spread), f(halves),
        b(gather_c), b(gather_c.T),
    ]


def body(
    total_facets, blocks, rows, chans, slots,
    image_ref, dual_ref, weight_ref, kern_ref, list_ref, count_ref, vis_hbm,
    fwd_a, fwd_b, inv_t, inv_l, twist, flip, spread, halves, gather_c, spread_c,
    next_ref, out_ref,
    grid_ref, full_ref, vis_ref, part_ref, place_ref, back_ref, fold_ref, sib_ref, mine_ref,
    land_ref, ybuf, ubuf, usmall, kfwd, kadj, halo_send, halo_in, ext_ref, ext_send, ext_in,
    upd_ref, own_energy, energy_send, energy_in, pick_s, pos_s, rev_s,
    vis_sem, ag_send, ag_recv, sb_send, sb_recv, fw_send, fw_recv, xs_send, xs_recv,
    rs_send, rs_recv, misc_send, misc_recv,
):
    outer = image_ref.shape[1] // chans
    half = outer // 2
    tiles = half + 1
    nz = blocks // 2
    facet, vis, spec = (lax.axis_index(a) for a in ("facet", "vis", "spec"))
    z = vis // 2
    core = vis % 2
    place = core * nz + z
    position = facet * blocks + vis
    everyone = total_facets * blocks
    after = (position + 1) % everyone
    before = (position + everyone - 1) % everyone
    sibling = {"vis": z * 2 + 1 - core}
    partner = {"spec": 1 - spec}
    next_dev = {"facet": after // blocks, "vis": after % blocks}
    prev_dev = {"facet": before // blocks, "vis": before % blocks}

    def peer(step):
        return {"vis": ((z + step) % nz) * 2 + core}

    vis_copies = [
        pltpu.make_async_copy(vis_hbm.at[c], vis_ref.at[c], vis_sem.at[c]) for c in range(chans)
    ]
    for copy in vis_copies:
        copy.start()

    barrier = pltpu.get_barrier_semaphore()
    greet = [peer(j) for j in range(1, nz)] + [sibling, partner, next_dev, prev_dev]
    for who in greet:
        pl.semaphore_signal(barrier, inc=1, device_id=who, device_id_type=MESH)

    def first(r, _):
        y = nn(fwd_a[...], image_ref[r].astype(bf16))
        cos, sin = twist[0], twist[1]
        for c in range(chans):
            re = y[c * 2 * outer : c * 2 * outer + outer][None]
            im = y[c * 2 * outer + outer : (c + 1) * 2 * outer][None]
            tre = (re * cos + im * sin).reshape(lanes, lanes).astype(bf16)
            tim = (im * cos - re * sin).reshape(lanes, lanes).astype(bf16)
            base = pl.multiple_of(r * 2 * lanes, 2 * lanes)
            ybuf[c, :, pl.ds(base, lanes)] = tre
            ybuf[c, :, pl.ds(pl.multiple_of(base + lanes, lanes), lanes)] = tim
        return 0

    lax.fori_loop(0, rows, first, 0)
    for r in range(3):
        halo_send[r] = dual_ref[rows - 3 + r].astype(bf16)

    def remote(src, dst, send, recv, who):
        return pltpu.make_async_remote_copy(
            src_ref=src, dst_ref=dst, send_sem=send, recv_sem=recv, device_id=who,
            device_id_type=MESH,
        )

    pl.semaphore_wait(barrier, len(greet))
    pending = []
    ag, sb = {}, {}
    for c in range(chans):
        panel = nt(fwd_b[...], ybuf[c]).astype(bf16).reshape(tiles, 2 * rows, lanes)
        grid_ref[c, place] = panel
        for j in range(1, nz):
            ag[c, j] = remote(
                grid_ref.at[c, place], grid_ref.at[c, place],
                ag_send.at[c, j - 1], ag_recv.at[c, j - 1], peer(j),
            )
            ag[c, j].start()
        sb[c] = remote(
            grid_ref.at[c, place], grid_ref.at[c, place], sb_send.at[c], sb_recv.at[c], sibling
        )
        sb[c].start()
    halo = remote(halo_send, halo_in, misc_send.at[0], misc_recv.at[0], next_dev)
    halo.start()

    width_tiles = outer
    for s in range(slots):
        tile = list_ref[s]
        pick_s[s] = jnp.where(tile < half, tile, width_tiles + half - 1 - tile)

    def positions(t, _):
        other = lax.rem(width_tiles - t, width_tiles)
        here, there = jnp.int32(slots), jnp.int32(slots)
        for s in range(slots):
            here = jnp.where(list_ref[s] == t, s, here)
            there = jnp.where(list_ref[s] == other, s, there)
        pos_s[t] = here
        rev_s[t] = there
        return 0

    lax.fori_loop(0, tiles + 1, positions, 0)
    k_re, k_im = kern_ref[0], kern_ref[1]
    top = nn(spread[0], k_re) - nn(spread[1], k_im)
    low = nn(spread[0], k_im) + nn(spread[1], k_re)
    both = jnp.concatenate([top, low], axis=1)
    kadj[...] = both.astype(bf16)
    kfwd[...] = both.T.astype(bf16)
    part_ref[slots] = jnp.zeros(part_ref.shape[1:], bf16)
    count = count_ref[0]

    lane0 = lax.broadcasted_iota(jnp.int32, (1, 2 * rows, lanes), 2) == 0
    sign = jnp.where(
        lax.broadcasted_iota(jnp.int32, (1, 2 * rows, lanes), 1) < rows, 1.0, -1.0
    ).astype(f32)
    tall = blocks * 2 * rows
    meas = vis_ref.shape[3]

    fw, xs, rs = {}, {}, {}

    def scatter(c):
        xs[c].wait_recv()

        def add(s, _):
            theirs = sib_ref[c, s].astype(f32)
            mine_ref[c, s] = (fold_ref[c, core * nz + s].astype(f32) + theirs).astype(bf16)
            return 0

        lax.fori_loop(0, nz, add, 0)
        for j in range(1, nz):
            rs[c, j] = remote(
                mine_ref.at[c, (z + j) % nz], land_ref.at[c, j - 1],
                rs_send.at[c, j - 1], rs_recv.at[c, j - 1], peer(j),
            )
            rs[c, j].start()

    for c in range(chans):
        for j in range(1, nz):
            ag[c, j].wait_recv()
            slot = core * nz + (z + nz - j) % nz
            fw[c, j] = remote(
                grid_ref.at[c, slot], grid_ref.at[c, slot],
                fw_send.at[c, j - 1], fw_recv.at[c, j - 1], sibling,
            )
            fw[c, j].start()
        if c > 0:
            scatter(c - 1)
        sb[c].wait_recv()
        for j in range(1, nz):
            fw[c, j].wait_recv()
        vis_copies[c].wait()

        def unfold(s, _):
            g = grid_ref[c, s]
            full_ref[s, :half] = g[:half]
            back = nn(g[:half].reshape(half * 2 * rows, lanes), flip[...])
            back = back.reshape(half, 2 * rows, lanes)
            back = jnp.where(lane0, g[1:].astype(f32), back) * sign
            full_ref[s, half:] = back.astype(bf16)
            return 0

        lax.fori_loop(0, blocks, unfold, 0)

        def degrid(k, _):
            pair = [2 * k, 2 * k + 1]
            picked = [full_ref[:, pick_s[s]].reshape(tall, lanes) for s in pair]
            pred = nn(kfwd[...], jnp.concatenate(picked, axis=1))
            res = []
            for n, s in enumerate(pair):
                live = (s < count).astype(f32)
                data = vis_ref[c, :, s].reshape(2 * meas, lanes).astype(f32)
                res.append(((pred[:, n * lanes : (n + 1) * lanes] - data) * live).astype(bf16))
            adj = nn(kadj[...], jnp.concatenate(res, axis=1)).astype(bf16)
            for n, s in enumerate(pair):
                part_ref[s] = adj[:, n * lanes : (n + 1) * lanes]
            return 0

        lax.fori_loop(0, slots // 2, degrid, 0)

        def put(t, _):
            place_ref[:, t] = part_ref[pos_s[t]].reshape(blocks, 2 * rows, lanes)
            back_ref[:, t] = part_ref[rev_s[t]].reshape(blocks, 2 * rows, lanes)
            return 0

        lax.fori_loop(0, tiles + 1, put, 0)

        def fold(s, _):
            q = back_ref[s]
            back = nn(q[1:].reshape(tiles * 2 * rows, lanes), flip[...])
            back = back.reshape(tiles, 2 * rows, lanes)
            back = jnp.where(lane0, q[:tiles].astype(f32), back) * sign
            sums = (place_ref[s, :tiles].astype(f32) + back) * halves[...]
            fold_ref[c, s] = sums.astype(bf16)
            return 0

        lax.fori_loop(0, blocks, fold, 0)
        xs[c] = remote(
            fold_ref.at[c, pl.ds((1 - core) * nz, nz)], sib_ref.at[c],
            xs_send.at[c], xs_recv.at[c], sibling,
        )
        xs[c].start()
    scatter(chans - 1)

    for c in range(chans):
        sums = mine_ref[c, z].astype(f32)
        for j in range(1, nz):
            rs[c, j].wait_recv()
            sums = sums + land_ref[c, j - 1].astype(f32)
        flat = sums.astype(bf16).reshape(tiles * 2 * rows, lanes)
        usmall[...] = nn(inv_t[...], flat).reshape(rows, 2, outer, lanes)

        def turn(r, _):
            re, im = usmall[r, 0][None], usmall[r, 1][None]
            cos, sin = twist[0], twist[1]
            tre = (re * cos - im * sin).reshape(lanes, lanes).astype(bf16)
            tim = (re * sin + im * cos).reshape(lanes, lanes).astype(bf16)
            ubuf[r, :, c * 2 * lanes : c * 2 * lanes + lanes] = tre
            ubuf[r, :, c * 2 * lanes + lanes : (c + 1) * 2 * lanes] = tim
            return 0

        lax.fori_loop(0, rows, turn, 0)

    halo.wait_recv()
    has_before = (position > 0).astype(f32)
    has_after = (position < everyone - 1).astype(f32)

    def dual_at(r):
        return dual_ref[r] if r >= 0 else halo_in[r + 3].astype(f32) * has_before

    for r in range(rows):
        grad = nt(inv_l[...], ubuf[r])
        synth = high_taps[0] * dual_at(r)
        for j in range(1, 4):
            synth = synth + high_taps[j] * dual_at(r - j)
        old = image_ref[r]
        new = jnp.maximum(old - primal_step * (grad + synth), 0.0)
        next_ref[r] = new
        ext = 2.0 * new - old
        ext_ref[r] = ext
        if r < 3:
            ext_send[r] = ext.astype(bf16)
        if r == 2:
            rim = remote(ext_send, ext_in, misc_send.at[1], misc_recv.at[1], prev_dev)
            rim.start()

    def ext_at(r):
        return ext_ref[r] if r < rows else ext_in[r - rows].astype(f32) * has_after

    def energies(first_row, last_row, n):
        for r in range(first_row, last_row):
            detail = high_taps[0] * ext_at(r)
            for j in range(1, 4):
                detail = detail + high_taps[j] * ext_at(r + j)
            upd = dual_ref[r] + dual_step * detail
            upd_ref[r] = upd
            square = upd * upd
            hi = square.astype(bf16)
            lo = (square - hi.astype(f32)).astype(bf16)
            energy = nn(gather_c[...], hi) + nn(gather_c[...], lo)
            own_energy[r] = energy
            energy_send[r] = energy.astype(bf16)
        rng = pl.ds(first_row, last_row - first_row)
        copy = remote(
            energy_send.at[rng], energy_in.at[rng], misc_send.at[n], misc_recv.at[n], partner
        )
        copy.start()
        return copy

    def finish(first_row, last_row):
        for r in range(first_row, last_row):
            energy = own_energy[r] + energy_in[r].astype(f32)
            w = weight_ref[:, r, :]
            ratio = w / jnp.maximum(w, jnp.sqrt(energy))
            hi = ratio.astype(bf16)
            lo = (ratio - hi.astype(f32)).astype(bf16)
            out_ref[r] = upd_ref[r] * (nn(spread_c[...], hi) + nn(spread_c[...], lo))

    cut = rows - 3
    early = energies(0, cut, 2)
    rim.wait_recv()
    late = energies(cut, rows, 3)
    early.wait_recv()
    finish(0, cut)
    late.wait_recv()
    finish(cut, rows)

    for copy in [*ag.values(), *sb.values(), *fw.values(), *xs.values(), *rs.values()]:
        copy.wait_send()
    for copy in (halo, rim, early, late):
        copy.wait_send()


def per_device(image, wavelet_dual, weights, kernels, vis_data, tile_list, tile_count):
    rows, chans, width = image.shape
    outer = width // lanes
    facets, blocks = lax.axis_size("facet"), lax.axis_size("vis")
    nz = blocks // 2
    slots = tile_list.shape[-1]
    meas = vis_data.shape[-2]
    tiles = outer // 2 + 1
    tall = blocks * 2 * rows

    def to_rows(x):
        x = x.reshape(rows, chans, outer, lanes).transpose(0, 2, 1, 3)
        return x.reshape(rows, outer * chans, lanes)

    def from_rows(x):
        x = x.reshape(rows, outer, chans, lanes).transpose(0, 2, 1, 3)
        return x.reshape(rows, chans, width)

    consts = tables(rows, chans, width, blocks)
    vmem = pl.BlockSpec(memory_space=pltpu.VMEM)
    smem = pl.BlockSpec(memory_space=pltpu.SMEM)
    sheet = (outer * chans, lanes)
    panel = (tiles, 2 * rows, lanes)
    dma = pltpu.SemaphoreType.DMA
    hop = (chans, nz - 1)
    scratch = [
        pltpu.VMEM((chans, blocks) + panel, bf16),
        pltpu.VMEM((blocks, outer, 2 * rows, lanes), bf16),
        pltpu.VMEM((chans, 2, slots, meas, lanes), bf16),
        pltpu.VMEM((slots + 1, tall, lanes), bf16),
        pltpu.VMEM((blocks, tiles + 1, 2 * rows, lanes), bf16),
        pltpu.VMEM((blocks, tiles + 1, 2 * rows, lanes), bf16),
        pltpu.VMEM((chans, blocks) + panel, bf16),
        pltpu.VMEM((chans, nz) + panel, bf16),
        pltpu.VMEM((chans, nz) + panel, bf16),
        pltpu.VMEM((chans, nz - 1) + panel, bf16),
        pltpu.VMEM((chans, lanes, rows * 2 * lanes), bf16),
        pltpu.VMEM((rows, lanes, chans * 2 * lanes), bf16),
        pltpu.VMEM((rows, 2, outer, lanes), f32),
        pltpu.VMEM((2 * meas, tall), bf16),
        pltpu.VMEM((tall, 2 * meas), bf16),
        pltpu.VMEM((3,) + sheet, bf16),
        pltpu.VMEM((3,) + sheet, bf16),
        pltpu.VMEM((rows,) + sheet, f32),
        pltpu.VMEM((3,) + sheet, bf16),
        pltpu.VMEM((3,) + sheet, bf16),
        pltpu.VMEM((rows,) + sheet, f32),
        pltpu.VMEM((rows, outer, lanes), f32),
        pltpu.VMEM((rows, outer, lanes), bf16),
        pltpu.VMEM((rows, outer, lanes), bf16),
        pltpu.SMEM((slots,), jnp.int32),
        pltpu.SMEM((tiles + 1,), jnp.int32),
        pltpu.SMEM((tiles + 1,), jnp.int32),
        dma((chans,)), dma(hop), dma(hop), dma((chans,)), dma((chans,)), dma(hop), dma(hop),
        dma((chans,)), dma((chans,)), dma(hop), dma(hop), dma((4,)), dma((4,)),
    ]
    shape = jax.ShapeDtypeStruct((rows,) + sheet, f32)
    new, dual = pl.pallas_call(
        functools.partial(body, facets, blocks, rows, chans, slots),
        out_shape=(shape, shape),
        in_specs=[vmem] * 4 + [smem] * 2 + [pl.BlockSpec(memory_space=pl.ANY)]
        + [vmem] * len(consts),
        out_specs=(vmem, vmem),
        scratch_shapes=scratch,
        compiler_params=pltpu.CompilerParams(
            collective_id=0, has_side_effects=True, vmem_limit_bytes=52 * 2**20
        ),
    )(
        to_rows(image),
        to_rows(wavelet_dual),
        weights.reshape(rows, outer, lanes).transpose(1, 0, 2),
        jnp.swapaxes(kernels[0, 0], 1, 2),
        tile_list.reshape(slots),
        tile_count.reshape(1),
        vis_data[0, 0],
        *consts,
    )
    return from_rows(new), from_rows(dual)


def solution(mesh):
    return jax.shard_map(
        per_device,
        mesh=mesh,
        in_specs=(
            P(("facet", "vis"), "spec", None),
            P(("facet", "vis"), "spec", None),
            P(("facet", "vis"), None),
            P("facet", "vis", None, None, None),
            P("facet", "vis", "spec", None, None, None, None),
            P("facet", "vis", None),
            P("facet", "vis"),
        ),
        out_specs=(P(("facet", "vis"), "spec", None), P(("facet", "vis"), "spec", None)),
        check_vma=False,
    )
```

```python
import functools
import math

import jax
import jax.numpy as jnp
import numpy as np
from jax import lax
from jax.experimental import pallas as pl
from jax.experimental.pallas import tpu as pltpu
from jax.sharding import PartitionSpec as P

MESH = pl.DeviceIdType.MESH
root_three = math.sqrt(3.0)
norm_factor = 4.0 * math.sqrt(2.0)
low_taps = [
    (1.0 + root_three) / norm_factor,
    (3.0 + root_three) / norm_factor,
    (3.0 - root_three) / norm_factor,
    (1.0 - root_three) / norm_factor,
]
high_taps = [low_taps[3], -low_taps[2], low_taps[1], -low_taps[0]]
primal_step = 0.2
dual_step = 0.5
lanes = 128
bf16 = jnp.bfloat16
f32 = jnp.float32


def nn(a, b):
    return jnp.dot(a, b, preferred_element_type=f32)


def nt(a, b):
    return lax.dot_general(a, b, (((1,), (1,)), ((), ())), preferred_element_type=f32)


def tables(rows, chans, width, blocks):
    outer = width // lanes
    half = outer // 2
    tiles = half + 1
    scale = 1.0 / math.sqrt(width)
    one = np.arange(outer)
    small = 2.0 * np.pi * (np.outer(one, one) % outer) / outer
    cos_s, sin_s = np.cos(small), np.sin(small)
    eye_c, eye_r = np.eye(chans), np.eye(rows)
    parts = np.stack([cos_s, -sin_s]) * scale
    fwd_a = np.einsum("pla,cd->cplad", parts, eye_c).reshape(chans * 2 * outer, outer * chans)
    angle = 2.0 * np.pi * (np.outer(np.arange(tiles), np.arange(lanes)) % outer) / outer
    cos_t, sin_t = np.cos(angle), np.sin(angle)
    mix = np.array([[cos_t, sin_t], [-sin_t, cos_t]])
    fwd_b = np.einsum("iptb,rs->tirspb", mix, eye_r).reshape(tiles * 2 * rows, rows * 2 * lanes)
    cos_o, sin_o = cos_t[:, :outer], sin_t[:, :outer]
    mix = np.array([[cos_o, -sin_o], [sin_o, cos_o]])
    inv_t = np.einsum("pitb,rs->rpbtis", mix, eye_r).reshape(rows * 2 * outer, tiles * 2 * rows)
    angle = 2.0 * np.pi * (np.outer(one, np.arange(lanes)) % outer) / outer
    parts = np.stack([np.cos(angle), -np.sin(angle)]) * scale
    inv_l = np.einsum("pal,cd->acdpl", parts, eye_c).reshape(outer * chans, chans * 2 * lanes)
    twist = 2.0 * np.pi * np.outer(np.arange(lanes), np.arange(lanes)) / width
    twist = np.stack([np.cos(twist), np.sin(twist)]).reshape(2, lanes // outer, outer, lanes)
    flip = np.zeros((lanes, lanes))
    for col in range(1, lanes):
        flip[lanes - col, col] = 1.0
    spread = np.zeros((2, blocks, 2, rows, blocks * rows))
    for shard in range(blocks):
        place = (shard % 2) * (blocks // 2) + shard // 2
        for row in range(rows):
            for part in range(2):
                spread[part, place, part, row, shard * rows + row] = 1.0
    spread = spread.reshape(2, blocks * 2 * rows, blocks * rows)
    halves = np.ones((tiles, 2 * rows, lanes))
    halves[0, :, 0] = 0.5
    halves[half, :, 1:] = 0.0
    halves[half, :, 0] = 0.5
    gather_c = np.kron(np.eye(outer), np.ones((1, chans)))

    def b(x):
        return jnp.asarray(x.astype(np.float32), bf16)

    def f(x):
        return jnp.asarray(x.astype(np.float32))

    return [
        b(fwd_a), b(fwd_b), b(inv_t), b(inv_l), f(twist), b(flip), b(spread), f(halves),
        b(gather_c), b(gather_c.T),
    ]


def body(
    loads, total_facets, blocks, rows, chans, slots,
    *refs,
):
    names = len(loads) + 1
    sources, vis_hbm = refs[: names - 1], refs[names - 1]
    next_ref, out_ref = refs[names : names + 2]
    held = refs[names + 2 : 2 * names + 1]
    (
        image_ref, dual_ref, weight_ref, kern_ref, list_ref, count_ref,
        fwd_a, fwd_b, inv_t, inv_l, twist, flip, spread, halves, gather_c, spread_c,
    ) = held
    load_sem = refs[2 * names + 1]
    (
    grid_ref, full_ref, vis_ref, part_ref, place_ref, back_ref, fold_ref, sib_ref, mine_ref,
    land_ref, ybuf, ubuf, usmall, kfwd, kadj, halo_send, halo_in, ext_ref, ext_send, ext_in,
    upd_ref, own_energy, energy_send, energy_in, pick_s, pos_s, rev_s,
    vis_sem, ag_send, ag_recv, sb_send, sb_recv, fw_send, fw_recv, xs_send, xs_recv,
    rs_send, rs_recv, misc_send, misc_recv, sum_ref, relay_ref,
    rl_send, relay_send, relay_recv,
    ) = refs[2 * names + 2 :]
    outer = image_ref.shape[1] // chans
    half = outer // 2
    tiles = half + 1
    nz = blocks // 2
    facet, vis, spec = (lax.axis_index(a) for a in ("facet", "vis", "spec"))
    z = vis // 2
    core = vis % 2
    place = core * nz + z
    position = facet * blocks + vis
    everyone = total_facets * blocks
    after = (position + 1) % everyone
    before = (position + everyone - 1) % everyone
    sibling = {"vis": z * 2 + 1 - core}
    partner = {"spec": 1 - spec}
    next_dev = {"facet": after // blocks, "vis": after % blocks}
    prev_dev = {"facet": before // blocks, "vis": before % blocks}

    def to(step):
        if nz == 4:
            return [z + 1 - 2 * (z % 2), (z + 2) % 4, 3 - z][step - 1]
        return (z + step) % nz

    def source(step):
        return to(step) if nz == 4 else (z + nz - step) % nz

    def peer(step):
        return {"vis": to(step) * 2 + core}

    short = nz == 4
    inner = z % 3 != 0

    loading = [
        pltpu.make_async_copy(src, dst, load_sem.at[n])
        for n, (src, dst) in enumerate(zip(sources, held))
    ]
    head, middle, last = [0, 6, 10, 7, 1], [3, 12, 4, 5, 11, 13], [8, 9, 2, 14, 15]
    for n in head + middle:
        loading[n].start()
    vis_copies = [
        pltpu.make_async_copy(vis_hbm.at[c], vis_ref.at[c], vis_sem.at[c]) for c in range(chans)
    ]
    for copy in vis_copies:
        copy.start()
    for n in last:
        loading[n].start()

    barrier = pltpu.get_barrier_semaphore()
    greet = [peer(j) for j in range(1, nz)] + [sibling, partner, next_dev, prev_dev]
    for who in greet:
        pl.semaphore_signal(barrier, inc=1, device_id=who, device_id_type=MESH)

    for n in head:
        loading[n].wait()

    def first(r, _):
        y = nn(fwd_a[...], image_ref[r].astype(bf16))
        cos, sin = twist[0], twist[1]
        for c in range(chans):
            re = y[c * 2 * outer : c * 2 * outer + outer][None]
            im = y[c * 2 * outer + outer : (c + 1) * 2 * outer][None]
            tre = (re * cos + im * sin).reshape(lanes, lanes).astype(bf16)
            tim = (im * cos - re * sin).reshape(lanes, lanes).astype(bf16)
            base = pl.multiple_of(r * 2 * lanes, 2 * lanes)
            ybuf[c, :, pl.ds(base, lanes)] = tre
            ybuf[c, :, pl.ds(pl.multiple_of(base + lanes, lanes), lanes)] = tim
        return 0

    lax.fori_loop(0, rows, first, 0)
    for r in range(3):
        halo_send[r] = dual_ref[rows - 3 + r].astype(bf16)

    def remote(src, dst, send, recv, who):
        return pltpu.make_async_remote_copy(
            src_ref=src, dst_ref=dst, send_sem=send, recv_sem=recv, device_id=who,
            device_id_type=MESH,
        )

    pl.semaphore_wait(barrier, len(greet))
    pending = []
    ag, sb = {}, {}
    for c in range(chans):
        panel = nt(fwd_b[...], ybuf[c]).astype(bf16).reshape(tiles, 2 * rows, lanes)
        grid_ref[c, place] = panel
        for j in range(1, nz):
            ag[c, j] = remote(
                grid_ref.at[c, place], grid_ref.at[c, place],
                ag_send.at[c, j - 1], ag_recv.at[c, j - 1], peer(j),
            )
            if short and j == 3:
                pl.when(inner)(ag[c, j].start)
            else:
                ag[c, j].start()
        sb[c] = remote(
            grid_ref.at[c, place], grid_ref.at[c, place], sb_send.at[c], sb_recv.at[c], sibling
        )
        sb[c].start()
    halo = remote(halo_send, halo_in, misc_send.at[0], misc_recv.at[0], next_dev)
    halo.start()

    width_tiles = outer
    for n in middle:
        loading[n].wait()
    for s in range(slots):
        tile = list_ref[s]
        pick_s[s] = jnp.where(tile < half, tile, width_tiles + half - 1 - tile)

    def positions(t, _):
        other = lax.rem(width_tiles - t, width_tiles)
        here, there = jnp.int32(slots), jnp.int32(slots)
        for s in range(slots):
            here = jnp.where(list_ref[s] == t, s, here)
            there = jnp.where(list_ref[s] == other, s, there)
        pos_s[t] = here
        rev_s[t] = there
        return 0

    lax.fori_loop(0, tiles + 1, positions, 0)
    k_re, k_im = kern_ref[0], kern_ref[1]
    top = nn(spread[0], k_re) - nn(spread[1], k_im)
    low = nn(spread[0], k_im) + nn(spread[1], k_re)
    both = jnp.concatenate([top, low], axis=1)
    kadj[...] = both.astype(bf16)
    kfwd[...] = both.T.astype(bf16)
    part_ref[slots] = jnp.zeros(part_ref.shape[1:], bf16)
    count = count_ref[0]

    lane0 = lax.broadcasted_iota(jnp.int32, (1, 2 * rows, lanes), 2) == 0
    sign = jnp.where(
        lax.broadcasted_iota(jnp.int32, (1, 2 * rows, lanes), 1) < rows, 1.0, -1.0
    ).astype(f32)
    tall = blocks * 2 * rows
    meas = vis_ref.shape[3]

    fw, xs, rs, extra, relayed = {}, {}, {}, {}, {}

    def relay(c):
        if not short:
            return

        @pl.when(inner)
        def _():
            extra[c].wait_recv()
            there = to(2)
            both = mine_ref[c, there].astype(f32) + relay_ref[c].astype(f32)
            mine_ref[c, there] = both.astype(bf16)
            rs[c, 2].start()

    def scatter(c):
        xs[c].wait_recv()

        def add(s, _):
            theirs = sib_ref[c, s].astype(f32)
            mine_ref[c, s] = (fold_ref[c, core * nz + s].astype(f32) + theirs).astype(bf16)
            return 0

        lax.fori_loop(0, nz, add, 0)
        for j in range(1, nz):
            rs[c, j] = remote(
                mine_ref.at[c, to(j)], land_ref.at[c, j - 1],
                rs_send.at[c, j - 1], rs_recv.at[c, j - 1], peer(j),
            )
            if not short:
                rs[c, j].start()
        if short:
            extra[c] = remote(
                mine_ref.at[c, to(3)], relay_ref.at[c], relay_send.at[c], relay_recv.at[c], peer(1)
            )
            pl.when(jnp.logical_not(inner))(extra[c].start)
            rs[c, 1].start()
            pl.when(jnp.logical_not(inner))(rs[c, 2].start)
            pl.when(inner)(rs[c, 3].start)

    def pass_on(c, steps):
        for j in steps:
            ag[c, j].wait_recv()
            slot = core * nz + source(j)
            if short and j == 2:
                relayed[c] = remote(
                    grid_ref.at[c, slot], grid_ref.at[c, slot],
                    rl_send.at[c], ag_recv.at[c, 2], peer(1),
                )
                pl.when(inner)(relayed[c].start)
            fw[c, j] = remote(
                grid_ref.at[c, slot], grid_ref.at[c, slot],
                fw_send.at[c, j - 1], fw_recv.at[c, j - 1], sibling,
            )
            fw[c, j].start()

    for c in range(chans):
        pass_on(c, (2, 1) if short else range(1, nz))
        if c > 0:
            scatter(c - 1)
        if short:
            pass_on(c, (3,))
        sb[c].wait_recv()
        for j in range(1, nz):
            fw[c, j].wait_recv()
        vis_copies[c].wait()

        def unfold(s, _):
            g = grid_ref[c, s]
            full_ref[s, :half] = g[:half]
            back = nn(g[:half].reshape(half * 2 * rows, lanes), flip[...])
            back = back.reshape(half, 2 * rows, lanes)
            back = jnp.where(lane0, g[1:].astype(f32), back) * sign
            full_ref[s, half:] = back.astype(bf16)
            return 0

        lax.fori_loop(0, blocks, unfold, 0)

        def degrid(k, _):
            pair = [2 * k, 2 * k + 1]
            picked = [full_ref[:, pick_s[s]].reshape(tall, lanes) for s in pair]
            pred = nn(kfwd[...], jnp.concatenate(picked, axis=1))
            res = []
            for n, s in enumerate(pair):
                live = (s < count).astype(f32)
                data = vis_ref[c, :, s].reshape(2 * meas, lanes).astype(f32)
                res.append(((pred[:, n * lanes : (n + 1) * lanes] - data) * live).astype(bf16))
            adj = nn(kadj[...], jnp.concatenate(res, axis=1)).astype(bf16)
            for n, s in enumerate(pair):
                part_ref[s] = adj[:, n * lanes : (n + 1) * lanes]
            return 0

        lax.fori_loop(0, slots // 2, degrid, 0)

        def put(t, _):
            place_ref[:, t] = part_ref[pos_s[t]].reshape(blocks, 2 * rows, lanes)
            back_ref[:, t] = part_ref[rev_s[t]].reshape(blocks, 2 * rows, lanes)
            return 0

        lax.fori_loop(0, tiles + 1, put, 0)

        def fold(s, _):
            q = back_ref[s]
            back = nn(q[1:].reshape(tiles * 2 * rows, lanes), flip[...])
            back = back.reshape(tiles, 2 * rows, lanes)
            back = jnp.where(lane0, q[:tiles].astype(f32), back) * sign
            sums = (place_ref[s, :tiles].astype(f32) + back) * halves[...]
            fold_ref[c, s] = sums.astype(bf16)
            return 0

        lax.fori_loop(0, blocks, fold, 0)
        xs[c] = remote(
            fold_ref.at[c, pl.ds((1 - core) * nz, nz)], sib_ref.at[c],
            xs_send.at[c], xs_recv.at[c], sibling,
        )
        xs[c].start()
        if c > 0:
            relay(c - 1)
    scatter(chans - 1)
    relay(chans - 1)
    for n in last:
        loading[n].wait()

    for c in range(chans):
        sums = mine_ref[c, z].astype(f32)
        for j in range(1, 3 if short else nz):
            rs[c, j].wait_recv()
            sums = sums + land_ref[c, j - 1].astype(f32)
        sum_ref[...] = sums
        if short:

            @pl.when(inner)
            def _():
                rs[c, 3].wait_recv()
                sum_ref[...] += land_ref[c, 2].astype(f32)

        flat = sum_ref[...].astype(bf16).reshape(tiles * 2 * rows, lanes)
        usmall[...] = nn(inv_t[...], flat).reshape(rows, 2, outer, lanes)

        def turn(r, _):
            re, im = usmall[r, 0][None], usmall[r, 1][None]
            cos, sin = twist[0], twist[1]
            tre = (re * cos - im * sin).reshape(lanes, lanes).astype(bf16)
            tim = (re * sin + im * cos).reshape(lanes, lanes).astype(bf16)
            ubuf[r, :, c * 2 * lanes : c * 2 * lanes + lanes] = tre
            ubuf[r, :, c * 2 * lanes + lanes : (c + 1) * 2 * lanes] = tim
            return 0

        lax.fori_loop(0, rows, turn, 0)

    halo.wait_recv()
    has_before = (position > 0).astype(f32)
    has_after = (position < everyone - 1).astype(f32)

    def dual_at(r):
        return dual_ref[r] if r >= 0 else halo_in[r + 3].astype(f32) * has_before

    for r in range(rows):
        grad = nt(inv_l[...], ubuf[r])
        synth = high_taps[0] * dual_at(r)
        for j in range(1, 4):
            synth = synth + high_taps[j] * dual_at(r - j)
        old = image_ref[r]
        new = jnp.maximum(old - primal_step * (grad + synth), 0.0)
        next_ref[r] = new
        ext = 2.0 * new - old
        ext_ref[r] = ext
        if r < 3:
            ext_send[r] = ext.astype(bf16)
        if r == 2:
            rim = remote(ext_send, ext_in, misc_send.at[1], misc_recv.at[1], prev_dev)
            rim.start()

    def ext_at(r):
        return ext_ref[r] if r < rows else ext_in[r - rows].astype(f32) * has_after

    def energies(first_row, last_row, n):
        for r in range(first_row, last_row):
            detail = high_taps[0] * ext_at(r)
            for j in range(1, 4):
                detail = detail + high_taps[j] * ext_at(r + j)
            upd = dual_ref[r] + dual_step * detail
            upd_ref[r] = upd
            square = upd * upd
            hi = square.astype(bf16)
            lo = (square - hi.astype(f32)).astype(bf16)
            energy = nn(gather_c[...], hi) + nn(gather_c[...], lo)
            own_energy[r] = energy
            energy_send[r] = energy.astype(bf16)
        rng = pl.ds(first_row, last_row - first_row)
        copy = remote(
            energy_send.at[rng], energy_in.at[rng], misc_send.at[n], misc_recv.at[n], partner
        )
        copy.start()
        return copy

    def finish(first_row, last_row):
        for r in range(first_row, last_row):
            energy = own_energy[r] + energy_in[r].astype(f32)
            w = weight_ref[:, r, :]
            ratio = w / jnp.maximum(w, jnp.sqrt(energy))
            hi = ratio.astype(bf16)
            lo = (ratio - hi.astype(f32)).astype(bf16)
            out_ref[r] = upd_ref[r] * (nn(spread_c[...], hi) + nn(spread_c[...], lo))

    cut = rows - 3
    early = energies(0, cut, 2)
    rim.wait_recv()
    late = energies(cut, rows, 3)
    early.wait_recv()
    finish(0, cut)
    late.wait_recv()
    finish(cut, rows)

    some = []
    for copies in (ag, rs):
        for (c, j), copy in copies.items():
            if short and j == 3:
                some.append(copy)
            else:
                copy.wait_send()
    for copy in [*sb.values(), *fw.values(), *xs.values()]:
        copy.wait_send()
    if short:

        @pl.when(inner)
        def _():
            for copy in [*some, *relayed.values()]:
                copy.wait_send()

        @pl.when(jnp.logical_not(inner))
        def _():
            for copy in extra.values():
                copy.wait_send()

    for copy in (halo, rim, early, late):
        copy.wait_send()


def per_device(image, wavelet_dual, weights, kernels, vis_data, tile_list, tile_count):
    rows, chans, width = image.shape
    outer = width // lanes
    facets, blocks = lax.axis_size("facet"), lax.axis_size("vis")
    nz = blocks // 2
    slots = tile_list.shape[-1]
    meas = vis_data.shape[-2]
    tiles = outer // 2 + 1
    tall = blocks * 2 * rows

    def to_rows(x):
        x = x.reshape(rows, chans, outer, lanes).transpose(0, 2, 1, 3)
        return x.reshape(rows, outer * chans, lanes)

    def from_rows(x):
        x = x.reshape(rows, outer, chans, lanes).transpose(0, 2, 1, 3)
        return x.reshape(rows, chans, width)

    consts = tables(rows, chans, width, blocks)
    vmem = pl.BlockSpec(memory_space=pltpu.VMEM)
    sheet = (outer * chans, lanes)
    panel = (tiles, 2 * rows, lanes)
    dma = pltpu.SemaphoreType.DMA
    hop = (chans, nz - 1)
    scratch = [
        pltpu.VMEM((chans, blocks) + panel, bf16),
        pltpu.VMEM((blocks, outer, 2 * rows, lanes), bf16),
        pltpu.VMEM((chans, 2, slots, meas, lanes), bf16),
        pltpu.VMEM((slots + 1, tall, lanes), bf16),
        pltpu.VMEM((blocks, tiles + 1, 2 * rows, lanes), bf16),
        pltpu.VMEM((blocks, tiles + 1, 2 * rows, lanes), bf16),
        pltpu.VMEM((chans, blocks) + panel, bf16),
        pltpu.VMEM((chans, nz) + panel, bf16),
        pltpu.VMEM((chans, nz) + panel, bf16),
        pltpu.VMEM((chans, nz - 1) + panel, bf16),
        pltpu.VMEM((chans, lanes, rows * 2 * lanes), bf16),
        pltpu.VMEM((rows, lanes, chans * 2 * lanes), bf16),
        pltpu.VMEM((rows, 2, outer, lanes), f32),
        pltpu.VMEM((2 * meas, tall), bf16),
        pltpu.VMEM((tall, 2 * meas), bf16),
        pltpu.VMEM((3,) + sheet, bf16),
        pltpu.VMEM((3,) + sheet, bf16),
        pltpu.VMEM((rows,) + sheet, f32),
        pltpu.VMEM((3,) + sheet, bf16),
        pltpu.VMEM((3,) + sheet, bf16),
        pltpu.VMEM((rows,) + sheet, f32),
        pltpu.VMEM((rows, outer, lanes), f32),
        pltpu.VMEM((rows, outer, lanes), bf16),
        pltpu.VMEM((rows, outer, lanes), bf16),
        pltpu.SMEM((slots,), jnp.int32),
        pltpu.SMEM((tiles + 1,), jnp.int32),
        pltpu.SMEM((tiles + 1,), jnp.int32),
        dma((chans,)), dma(hop), dma(hop), dma((chans,)), dma((chans,)), dma(hop), dma(hop),
        dma((chans,)), dma((chans,)), dma(hop), dma(hop), dma((4,)), dma((4,)),
        pltpu.VMEM(panel, f32),
        pltpu.VMEM((chans,) + panel, bf16),
        dma((chans,)), dma((chans,)), dma((chans,)),
    ]
    operands = [
        to_rows(image),
        to_rows(wavelet_dual),
        weights.reshape(rows, outer, lanes).transpose(1, 0, 2),
        jnp.swapaxes(kernels[0, 0], 1, 2),
        tile_list.reshape(slots),
        tile_count.reshape(1),
        *consts,
    ]
    held = [
        (pltpu.SMEM if x.dtype == jnp.int32 else pltpu.VMEM)(x.shape, x.dtype) for x in operands
    ]
    scratch = [*held, dma((len(operands),)), *scratch]
    shape = jax.ShapeDtypeStruct((rows,) + sheet, f32)
    new, dual = pl.pallas_call(
        functools.partial(body, operands, facets, blocks, rows, chans, slots),
        out_shape=(shape, shape),
        in_specs=[pl.BlockSpec(memory_space=pltpu.HBM)] * (len(operands) + 1),
        out_specs=(vmem, vmem),
        scratch_shapes=scratch,
        compiler_params=pltpu.CompilerParams(
            collective_id=0, has_side_effects=True, vmem_limit_bytes=64 * 2**20
        ),
    )(*operands, vis_data[0, 0])
    return from_rows(new), from_rows(dual)


def solution(mesh):
    return jax.shard_map(
        per_device,
        mesh=mesh,
        in_specs=(
            P(("facet", "vis"), "spec", None),
            P(("facet", "vis"), "spec", None),
            P(("facet", "vis"), None),
            P("facet", "vis", None, None, None),
            P("facet", "vis", "spec", None, None, None, None),
            P("facet", "vis", None),
            P("facet", "vis"),
        ),
        out_specs=(P(("facet", "vis"), "spec", None), P(("facet", "vis"), "spec", None)),
        check_vma=False,
    )
```

```python
import functools
import math

import jax
import jax.numpy as jnp
import numpy as np
from jax import lax
from jax.experimental import pallas as pl
from jax.experimental.pallas import tpu as pltpu
from jax.sharding import PartitionSpec as P

MESH = pl.DeviceIdType.MESH
root_three = math.sqrt(3.0)
norm_factor = 4.0 * math.sqrt(2.0)
low_taps = [
    (1.0 + root_three) / norm_factor,
    (3.0 + root_three) / norm_factor,
    (3.0 - root_three) / norm_factor,
    (1.0 - root_three) / norm_factor,
]
high_taps = [low_taps[3], -low_taps[2], low_taps[1], -low_taps[0]]
primal_step = 0.2
dual_step = 0.5
lanes = 128
bf16 = jnp.bfloat16
f32 = jnp.float32


def nn(a, b):
    return jnp.dot(a, b, preferred_element_type=f32)


def nt(a, b):
    return lax.dot_general(a, b, (((1,), (1,)), ((), ())), preferred_element_type=f32)


def tables(rows, chans, width, blocks):
    outer = width // lanes
    half = outer // 2
    tiles = half + 1
    scale = 1.0 / math.sqrt(width)
    one = np.arange(outer)
    small = 2.0 * np.pi * (np.outer(one, one) % outer) / outer
    cos_s, sin_s = np.cos(small), np.sin(small)
    eye_c, eye_r = np.eye(chans), np.eye(rows)
    parts = np.stack([cos_s, -sin_s]) * scale
    fwd_a = np.einsum("pla,cd->cplad", parts, eye_c).reshape(chans * 2 * outer, outer * chans)
    angle = 2.0 * np.pi * (np.outer(np.arange(tiles), np.arange(lanes)) % outer) / outer
    cos_t, sin_t = np.cos(angle), np.sin(angle)
    mix = np.array([[cos_t, sin_t], [-sin_t, cos_t]])
    fwd_b = np.einsum("iptb,rs->tirspb", mix, eye_r).reshape(tiles * 2 * rows, rows * 2 * lanes)
    cos_o, sin_o = cos_t[:, :outer], sin_t[:, :outer]
    mix = np.array([[cos_o, -sin_o], [sin_o, cos_o]])
    inv_t = np.einsum("pitb,rs->rpbtis", mix, eye_r).reshape(rows * 2 * outer, tiles * 2 * rows)
    angle = 2.0 * np.pi * (np.outer(one, np.arange(lanes)) % outer) / outer
    parts = np.stack([np.cos(angle), -np.sin(angle)]) * scale
    inv_l = np.einsum("pal,cd->acdpl", parts, eye_c).reshape(outer * chans, chans * 2 * lanes)
    twist = 2.0 * np.pi * np.outer(np.arange(lanes), np.arange(lanes)) / width
    twist = np.stack([np.cos(twist), np.sin(twist)]).reshape(2, lanes // outer, outer, lanes)
    flip = np.zeros((lanes, lanes))
    for col in range(1, lanes):
        flip[lanes - col, col] = 1.0
    spread = np.zeros((2, blocks, 2, rows, blocks * rows))
    for shard in range(blocks):
        place = (shard % 2) * (blocks // 2) + shard // 2
        for row in range(rows):
            for part in range(2):
                spread[part, place, part, row, shard * rows + row] = 1.0
    spread = spread.reshape(2, blocks * 2 * rows, blocks * rows)
    halves = np.ones((tiles, 2 * rows, lanes))
    halves[0, :, 0] = 0.5
    halves[half, :, 1:] = 0.0
    halves[half, :, 0] = 0.5
    gather_c = np.kron(np.eye(outer), np.ones((1, chans)))

    def b(x):
        return jnp.asarray(x.astype(np.float32), bf16)

    def f(x):
        return jnp.asarray(x.astype(np.float32))

    return [
        b(fwd_a), b(fwd_b), b(inv_t), b(inv_l), f(twist), b(flip), b(spread), f(halves),
        b(gather_c), b(gather_c.T),
    ]


def body(
    loads, total_facets, blocks, rows, chans, slots,
    *refs,
):
    names = len(loads) + 1
    sources, vis_hbm = refs[: names - 1], refs[names - 1]
    next_ref, out_ref = refs[names : names + 2]
    held = refs[names + 2 : 2 * names + 1]
    (
        image_ref, dual_ref, weight_ref, kern_ref, list_ref, count_ref,
        fwd_a, fwd_b, inv_t, inv_l, twist, flip, spread, halves, gather_c, spread_c,
    ) = held
    load_sem = refs[2 * names + 1]
    (
    grid_ref, full_ref, vis_ref, part_ref, place_ref, back_ref, fold_ref, sib_ref, mine_ref,
    land_ref, ybuf, ubuf, usmall, kfwd, kadj, halo_send, halo_in, ext_ref, ext_send, ext_in,
    upd_ref, own_energy, energy_send, energy_in, pick_s, pos_s, rev_s,
    vis_sem, ag_send, ag_recv, sb_send, sb_recv, fw_send, fw_recv, xs_send, xs_recv,
    rs_send, rs_recv, misc_send, misc_recv, sum_ref, relay_ref,
    rl_send, relay_send, relay_recv,
    ) = refs[2 * names + 2 :]
    outer = image_ref.shape[1] // chans
    half = outer // 2
    tiles = half + 1
    nz = blocks // 2
    facet, vis, spec = (lax.axis_index(a) for a in ("facet", "vis", "spec"))
    z = vis // 2
    core = vis % 2
    place = core * nz + z
    position = facet * blocks + vis
    everyone = total_facets * blocks
    after = (position + 1) % everyone
    before = (position + everyone - 1) % everyone
    sibling = {"vis": z * 2 + 1 - core}
    partner = {"spec": 1 - spec}
    next_dev = {"facet": after // blocks, "vis": after % blocks}
    prev_dev = {"facet": before // blocks, "vis": before % blocks}

    def to(step):
        if nz == 4:
            return [z + 1 - 2 * (z % 2), (z + 2) % 4, 3 - z][step - 1]
        return (z + step) % nz

    def source(step):
        return to(step) if nz == 4 else (z + nz - step) % nz

    def peer(step):
        return {"vis": to(step) * 2 + core}

    short = False
    ahead = min(4, chans)
    inner = z % 3 != 0

    loading = [
        pltpu.make_async_copy(src, dst, load_sem.at[n])
        for n, (src, dst) in enumerate(zip(sources, held))
    ]
    head, middle, last = [0, 6, 10, 7, 1], [3, 12, 4, 5, 11, 13], [8, 9, 2, 14, 15]
    for n in head + middle:
        loading[n].start()
    vis_copies = [
        pltpu.make_async_copy(vis_hbm.at[c], vis_ref.at[c], vis_sem.at[c]) for c in range(chans)
    ]
    for copy in vis_copies:
        copy.start()
    for n in last:
        loading[n].start()

    barrier = pltpu.get_barrier_semaphore()
    greet = [peer(j) for j in range(1, nz)] + [sibling, partner, next_dev, prev_dev]
    for who in greet:
        pl.semaphore_signal(barrier, inc=1, device_id=who, device_id_type=MESH)

    for n in head:
        loading[n].wait()

    def first(r, _):
        y = nn(fwd_a[...], image_ref[r].astype(bf16))
        cos, sin = twist[0], twist[1]
        for c in range(chans):
            re = y[c * 2 * outer : c * 2 * outer + outer][None]
            im = y[c * 2 * outer + outer : (c + 1) * 2 * outer][None]
            tre = (re * cos + im * sin).reshape(lanes, lanes).astype(bf16)
            tim = (im * cos - re * sin).reshape(lanes, lanes).astype(bf16)
            base = pl.multiple_of(r * 2 * lanes, 2 * lanes)
            ybuf[c, :, pl.ds(base, lanes)] = tre
            ybuf[c, :, pl.ds(pl.multiple_of(base + lanes, lanes), lanes)] = tim
        return 0

    lax.fori_loop(0, rows, first, 0)
    for r in range(3):
        halo_send[r] = dual_ref[rows - 3 + r].astype(bf16)

    def remote(src, dst, send, recv, who):
        return pltpu.make_async_remote_copy(
            src_ref=src, dst_ref=dst, send_sem=send, recv_sem=recv, device_id=who,
            device_id_type=MESH,
        )

    pl.semaphore_wait(barrier, len(greet))
    pending = []
    ag, sb = {}, {}
    first_lane = lax.broadcasted_iota(jnp.int32, (rows, lanes), 1) == 0

    def pack(panel):
        im = jnp.where(first_lane, panel[half, :rows], panel[0, rows:])
        return jnp.concatenate([jnp.concatenate([panel[0, :rows], im], 0)[None], panel[1:half]], 0)

    def unpack(panel):
        im = panel[0, rows:]
        low = jnp.concatenate([panel[0, :rows], jnp.where(first_lane, 0.0, im)], 0)
        middle = jnp.concatenate([jnp.where(first_lane, im, 0.0), jnp.zeros_like(im)], 0)
        return jnp.concatenate([low[None], panel[1:], middle[None]], 0)

    def send_panel(c):
        panel = nt(fwd_b[...], ybuf[c]).reshape(tiles, 2 * rows, lanes)
        grid_ref[c, place] = pack(panel).astype(bf16)
        for j in range(1, nz):
            ag[c, j] = remote(
                grid_ref.at[c, place], grid_ref.at[c, place],
                ag_send.at[c, j - 1], ag_recv.at[c, j - 1], peer(j),
            )
            if short and j == 3:
                pl.when(inner)(ag[c, j].start)
            else:
                ag[c, j].start()
        sb[c] = remote(
            grid_ref.at[c, place], grid_ref.at[c, place], sb_send.at[c], sb_recv.at[c], sibling
        )
        sb[c].start()

    for c in range(ahead):
        send_panel(c)
    halo = remote(halo_send, halo_in, misc_send.at[0], misc_recv.at[0], next_dev)
    halo.start()

    width_tiles = outer
    for n in middle:
        loading[n].wait()
    for s in range(slots):
        tile = list_ref[s]
        pick_s[s] = jnp.where(tile < half, tile, width_tiles + half - 1 - tile)

    def positions(t, _):
        other = lax.rem(width_tiles - t, width_tiles)
        here, there = jnp.int32(slots), jnp.int32(slots)
        for s in range(slots):
            here = jnp.where(list_ref[s] == t, s, here)
            there = jnp.where(list_ref[s] == other, s, there)
        pos_s[t] = here
        rev_s[t] = there
        return 0

    lax.fori_loop(0, tiles + 1, positions, 0)
    k_re, k_im = kern_ref[0], kern_ref[1]
    top = nn(spread[0], k_re) - nn(spread[1], k_im)
    low = nn(spread[0], k_im) + nn(spread[1], k_re)
    both = jnp.concatenate([top, low], axis=1)
    kadj[...] = both.astype(bf16)
    kfwd[...] = both.T.astype(bf16)
    part_ref[slots] = jnp.zeros(part_ref.shape[1:], bf16)
    count = count_ref[0]

    lane0 = lax.broadcasted_iota(jnp.int32, (1, 2 * rows, lanes), 2) == 0
    sign = jnp.where(
        lax.broadcasted_iota(jnp.int32, (1, 2 * rows, lanes), 1) < rows, 1.0, -1.0
    ).astype(f32)
    tall = blocks * 2 * rows
    meas = vis_ref.shape[3]

    fw, xs, rs, extra, relayed = {}, {}, {}, {}, {}

    def relay(c):
        if not short:
            return

        @pl.when(inner)
        def _():
            extra[c].wait_recv()
            there = to(2)
            both = mine_ref[c, there].astype(f32) + relay_ref[c].astype(f32)
            mine_ref[c, there] = both.astype(bf16)
            rs[c, 2].start()

    def scatter(c):
        xs[c].wait_recv()

        def add(s, _):
            theirs = sib_ref[c, s].astype(f32)
            mine_ref[c, s] = (fold_ref[c, core * nz + s].astype(f32) + theirs).astype(bf16)
            return 0

        lax.fori_loop(0, nz, add, 0)
        for j in range(1, nz):
            rs[c, j] = remote(
                mine_ref.at[c, to(j)], land_ref.at[c, j - 1],
                rs_send.at[c, j - 1], rs_recv.at[c, j - 1], peer(j),
            )
            if not short:
                rs[c, j].start()
        if short:
            extra[c] = remote(
                mine_ref.at[c, to(3)], relay_ref.at[c], relay_send.at[c], relay_recv.at[c], peer(1)
            )
            pl.when(jnp.logical_not(inner))(extra[c].start)
            rs[c, 1].start()
            pl.when(jnp.logical_not(inner))(rs[c, 2].start)
            pl.when(inner)(rs[c, 3].start)

    def pass_on(c, steps):
        for j in steps:
            ag[c, j].wait_recv()
            slot = core * nz + source(j)
            if short and j == 2:
                relayed[c] = remote(
                    grid_ref.at[c, slot], grid_ref.at[c, slot],
                    rl_send.at[c], ag_recv.at[c, 2], peer(1),
                )
                pl.when(inner)(relayed[c].start)
            fw[c, j] = remote(
                grid_ref.at[c, slot], grid_ref.at[c, slot],
                fw_send.at[c, j - 1], fw_recv.at[c, j - 1], sibling,
            )
            fw[c, j].start()

    for c in range(chans):
        pass_on(c, (2, 1) if short else range(1, nz))
        if c + ahead < chans:
            send_panel(c + ahead)
        if c > 0:
            scatter(c - 1)
        if short:
            pass_on(c, (3,))
        sb[c].wait_recv()
        for j in range(1, nz):
            fw[c, j].wait_recv()
        vis_copies[c].wait()

        def unfold(s, _):
            g = unpack(grid_ref[c, s].astype(f32))
            low = g[:half].astype(bf16)
            full_ref[s, :half] = low
            back = nn(low.reshape(half * 2 * rows, lanes), flip[...])
            back = back.reshape(half, 2 * rows, lanes)
            back = jnp.where(lane0, g[1:], back) * sign
            full_ref[s, half:] = back.astype(bf16)
            return 0

        lax.fori_loop(0, blocks, unfold, 0)

        def degrid(k, _):
            pair = [2 * k, 2 * k + 1]
            picked = [full_ref[:, pick_s[s]].reshape(tall, lanes) for s in pair]
            pred = nn(kfwd[...], jnp.concatenate(picked, axis=1))
            res = []
            for n, s in enumerate(pair):
                live = (s < count).astype(f32)
                data = vis_ref[c, :, s].reshape(2 * meas, lanes).astype(f32)
                res.append(((pred[:, n * lanes : (n + 1) * lanes] - data) * live).astype(bf16))
            adj = nn(kadj[...], jnp.concatenate(res, axis=1)).astype(bf16)
            for n, s in enumerate(pair):
                part_ref[s] = adj[:, n * lanes : (n + 1) * lanes]
            return 0

        lax.fori_loop(0, slots // 2, degrid, 0)

        def put(t, _):
            place_ref[:, t] = part_ref[pos_s[t]].reshape(blocks, 2 * rows, lanes)
            back_ref[:, t] = part_ref[rev_s[t]].reshape(blocks, 2 * rows, lanes)
            return 0

        lax.fori_loop(0, tiles + 1, put, 0)

        def fold(s, _):
            q = back_ref[s]
            back = nn(q[1:].reshape(tiles * 2 * rows, lanes), flip[...])
            back = back.reshape(tiles, 2 * rows, lanes)
            back = jnp.where(lane0, q[:tiles].astype(f32), back) * sign
            sums = (place_ref[s, :tiles].astype(f32) + back) * halves[...]
            fold_ref[c, s] = pack(sums).astype(bf16)
            return 0

        lax.fori_loop(0, blocks, fold, 0)
        xs[c] = remote(
            fold_ref.at[c, pl.ds((1 - core) * nz, nz)], sib_ref.at[c],
            xs_send.at[c], xs_recv.at[c], sibling,
        )
        xs[c].start()
        if c > 0:
            relay(c - 1)
    scatter(chans - 1)
    relay(chans - 1)
    for n in last:
        loading[n].wait()

    for c in range(chans):
        sums = mine_ref[c, z].astype(f32)
        for j in range(1, 3 if short else nz):
            rs[c, j].wait_recv()
            sums = sums + land_ref[c, j - 1].astype(f32)
        sum_ref[...] = sums
        if short:

            @pl.when(inner)
            def _():
                rs[c, 3].wait_recv()
                sum_ref[...] += land_ref[c, 2].astype(f32)

        flat = unpack(sum_ref[...]).astype(bf16).reshape(tiles * 2 * rows, lanes)
        usmall[...] = nn(inv_t[...], flat).reshape(rows, 2, outer, lanes)

        def turn(r, _):
            re, im = usmall[r, 0][None], usmall[r, 1][None]
            cos, sin = twist[0], twist[1]
            tre = (re * cos - im * sin).reshape(lanes, lanes).astype(bf16)
            tim = (re * sin + im * cos).reshape(lanes, lanes).astype(bf16)
            ubuf[r, :, c * 2 * lanes : c * 2 * lanes + lanes] = tre
            ubuf[r, :, c * 2 * lanes + lanes : (c + 1) * 2 * lanes] = tim
            return 0

        lax.fori_loop(0, rows, turn, 0)

    halo.wait_recv()
    has_before = (position > 0).astype(f32)
    has_after = (position < everyone - 1).astype(f32)

    def dual_at(r):
        return dual_ref[r] if r >= 0 else halo_in[r + 3].astype(f32) * has_before

    for r in range(rows):
        grad = nt(inv_l[...], ubuf[r])
        synth = high_taps[0] * dual_at(r)
        for j in range(1, 4):
            synth = synth + high_taps[j] * dual_at(r - j)
        old = image_ref[r]
        new = jnp.maximum(old - primal_step * (grad + synth), 0.0)
        next_ref[r] = new
        ext = 2.0 * new - old
        ext_ref[r] = ext
        if r < 3:
            ext_send[r] = ext.astype(bf16)
        if r == 2:
            rim = remote(ext_send, ext_in, misc_send.at[1], misc_recv.at[1], prev_dev)
            rim.start()

    def ext_at(r):
        return ext_ref[r] if r < rows else ext_in[r - rows].astype(f32) * has_after

    def energies(first_row, last_row, n):
        for r in range(first_row, last_row):
            detail = high_taps[0] * ext_at(r)
            for j in range(1, 4):
                detail = detail + high_taps[j] * ext_at(r + j)
            upd = dual_ref[r] + dual_step * detail
            upd_ref[r] = upd
            square = upd * upd
            hi = square.astype(bf16)
            lo = (square - hi.astype(f32)).astype(bf16)
            energy = nn(gather_c[...], hi) + nn(gather_c[...], lo)
            own_energy[r] = energy
            energy_send[r] = energy.astype(bf16)
        rng = pl.ds(first_row, last_row - first_row)
        copy = remote(
            energy_send.at[rng], energy_in.at[rng], misc_send.at[n], misc_recv.at[n], partner
        )
        copy.start()
        return copy

    def finish(first_row, last_row):
        for r in range(first_row, last_row):
            energy = own_energy[r] + energy_in[r].astype(f32)
            w = weight_ref[:, r, :]
            ratio = w / jnp.maximum(w, jnp.sqrt(energy))
            hi = ratio.astype(bf16)
            lo = (ratio - hi.astype(f32)).astype(bf16)
            out_ref[r] = upd_ref[r] * (nn(spread_c[...], hi) + nn(spread_c[...], lo))

    cut = rows - 3
    early = energies(0, cut, 2)
    rim.wait_recv()
    late = energies(cut, rows, 3)
    early.wait_recv()
    finish(0, cut)
    late.wait_recv()
    finish(cut, rows)

    some = []
    for copies in (ag, rs):
        for (c, j), copy in copies.items():
            if short and j == 3:
                some.append(copy)
            else:
                copy.wait_send()
    for copy in [*sb.values(), *fw.values(), *xs.values()]:
        copy.wait_send()
    if short:

        @pl.when(inner)
        def _():
            for copy in [*some, *relayed.values()]:
                copy.wait_send()

        @pl.when(jnp.logical_not(inner))
        def _():
            for copy in extra.values():
                copy.wait_send()

    for copy in (halo, rim, early, late):
        copy.wait_send()


def per_device(image, wavelet_dual, weights, kernels, vis_data, tile_list, tile_count):
    rows, chans, width = image.shape
    outer = width // lanes
    facets, blocks = lax.axis_size("facet"), lax.axis_size("vis")
    nz = blocks // 2
    slots = tile_list.shape[-1]
    meas = vis_data.shape[-2]
    tiles = outer // 2 + 1
    tall = blocks * 2 * rows

    def to_rows(x):
        x = x.reshape(rows, chans, outer, lanes).transpose(0, 2, 1, 3)
        return x.reshape(rows, outer * chans, lanes)

    def from_rows(x):
        x = x.reshape(rows, outer, chans, lanes).transpose(0, 2, 1, 3)
        return x.reshape(rows, chans, width)

    consts = tables(rows, chans, width, blocks)
    vmem = pl.BlockSpec(memory_space=pltpu.VMEM)
    sheet = (outer * chans, lanes)
    panel = (outer // 2, 2 * rows, lanes)
    dma = pltpu.SemaphoreType.DMA
    hop = (chans, nz - 1)
    scratch = [
        pltpu.VMEM((chans, blocks) + panel, bf16),
        pltpu.VMEM((blocks, outer, 2 * rows, lanes), bf16),
        pltpu.VMEM((chans, 2, slots, meas, lanes), bf16),
        pltpu.VMEM((slots + 1, tall, lanes), bf16),
        pltpu.VMEM((blocks, tiles + 1, 2 * rows, lanes), bf16),
        pltpu.VMEM((blocks, tiles + 1, 2 * rows, lanes), bf16),
        pltpu.VMEM((chans, blocks) + panel, bf16),
        pltpu.VMEM((chans, nz) + panel, bf16),
        pltpu.VMEM((chans, nz) + panel, bf16),
        pltpu.VMEM((chans, nz - 1) + panel, bf16),
        pltpu.VMEM((chans, lanes, rows * 2 * lanes), bf16),
        pltpu.VMEM((rows, lanes, chans * 2 * lanes), bf16),
        pltpu.VMEM((rows, 2, outer, lanes), f32),
        pltpu.VMEM((2 * meas, tall), bf16),
        pltpu.VMEM((tall, 2 * meas), bf16),
        pltpu.VMEM((3,) + sheet, bf16),
        pltpu.VMEM((3,) + sheet, bf16),
        pltpu.VMEM((rows,) + sheet, f32),
        pltpu.VMEM((3,) + sheet, bf16),
        pltpu.VMEM((3,) + sheet, bf16),
        pltpu.VMEM((rows,) + sheet, f32),
        pltpu.VMEM((rows, outer, lanes), f32),
        pltpu.VMEM((rows, outer, lanes), bf16),
        pltpu.VMEM((rows, outer, lanes), bf16),
        pltpu.SMEM((slots,), jnp.int32),
        pltpu.SMEM((tiles + 1,), jnp.int32),
        pltpu.SMEM((tiles + 1,), jnp.int32),
        dma((chans,)), dma(hop), dma(hop), dma((chans,)), dma((chans,)), dma(hop), dma(hop),
        dma((chans,)), dma((chans,)), dma(hop), dma(hop), dma((4,)), dma((4,)),
        pltpu.VMEM(panel, f32),
        pltpu.VMEM((chans,) + panel, bf16),
        dma((chans,)), dma((chans,)), dma((chans,)),
    ]
    operands = [
        to_rows(image),
        to_rows(wavelet_dual),
        weights.reshape(rows, outer, lanes).transpose(1, 0, 2),
        jnp.swapaxes(kernels[0, 0], 1, 2),
        tile_list.reshape(slots),
        tile_count.reshape(1),
        *consts,
    ]
    held = [
        (pltpu.SMEM if x.dtype == jnp.int32 else pltpu.VMEM)(x.shape, x.dtype) for x in operands
    ]
    scratch = [*held, dma((len(operands),)), *scratch]
    shape = jax.ShapeDtypeStruct((rows,) + sheet, f32)
    new, dual = pl.pallas_call(
        functools.partial(body, operands, facets, blocks, rows, chans, slots),
        out_shape=(shape, shape),
        in_specs=[pl.BlockSpec(memory_space=pltpu.HBM)] * (len(operands) + 1),
        out_specs=(vmem, vmem),
        scratch_shapes=scratch,
        compiler_params=pltpu.CompilerParams(
            collective_id=0, has_side_effects=True, vmem_limit_bytes=64 * 2**20
        ),
    )(*operands, vis_data[0, 0])
    return from_rows(new), from_rows(dual)


def solution(mesh):
    return jax.shard_map(
        per_device,
        mesh=mesh,
        in_specs=(
            P(("facet", "vis"), "spec", None),
            P(("facet", "vis"), "spec", None),
            P(("facet", "vis"), None),
            P("facet", "vis", None, None, None),
            P("facet", "vis", "spec", None, None, None, None),
            P("facet", "vis", None),
            P("facet", "vis"),
        ),
        out_specs=(P(("facet", "vis"), "spec", None), P(("facet", "vis"), "spec", None)),
        check_vma=False,
    )
```
